32 devices in a mesh: groups: 2 (over y), tm: 4 (over z), param: 4 (over x, core).
Axes of the slice: x: 2, y: 2, z: 4, core: 2. Of those that a mesh axis runs over, the one named last changes fastest.
Arguments:
- design: float32 [3, 512, 40960], P(None, ('groups', 'tm'), 'param'), parts along dimension 1, may hold values from -0.03125 to 0.03125
- filter_taps: float32 [3, 512], replicated, may hold values from -0.25 to 0.25
- probes: float32 [40960, 256], P('param', ('groups', 'tm')), parts along dimension 1, may hold values from -6 to 6
Outputs:
- normal_product: float32 [40960, 256], P('param', ('groups', 'tm')), parts along dimension 1
The draws below stay inside these ranges and needn't reach their ends.
There are 2 independent parts, one for each index of `groups`. The reference program is written for one: setup_inputs(seed, part) draws one part's arguments, and reference() takes and returns one part's arrays. A program takes and returns all parts, laid end to end along the dimension named above; an argument that names none is the same for every part. Nothing has to cross between parts.
All inputs are finite; a program needn't handle non-finite values.
Results may differ from the reference program's by a relative error of at most 0.000071.
Values sent between devices are 32-bit elements; how exact they have to be, the bound alone decides.
A program may use at most 128 MiB of HBM per device.

```python
import jax
import jax.numpy as jnp
from jax import lax

P_SIZE = 40960
COMP = 3
TAPS = 512
PROBES = 128
EPOCHS = 256


def block_levels(key, extent, cuts, least, largest):
    level = 1.0
    for axis_at, parts in cuts:
        draws = jax.random.uniform(jax.random.fold_in(jax.random.fold_in(key, 6), axis_at), (parts,), jnp.float32, least / len(cuts), largest / len(cuts))
        level = level * jnp.repeat(jnp.exp(draws), extent[axis_at] // parts).reshape((-1,) + (1,) * (len(extent) - 1 - axis_at))
    return level


def scatter_about(key, shape, scale, limit, split=(), dtype=jnp.bfloat16):
    values = jax.random.normal(key, shape, jnp.float32) * scale
    if len(split) > 0:
        values = block_levels(key, shape, split, -0.22, 0.18) * values
    return jnp.clip(values, min=-limit, max=limit).astype(dtype)


def setup_inputs(seed: int = 0, part: int = 0) -> dict:
    keys = jax.random.split(jax.random.key(seed), 4)
    own_keys = jax.random.split(jax.random.fold_in(keys[3], part), 4)
    return {
        "design": scatter_about(own_keys[0], (COMP, EPOCHS, P_SIZE), P_SIZE ** -0.5, 0.03125, ((1, 4), (2, 4)), jnp.float32),
        "filter_taps": scatter_about(keys[1], (COMP, TAPS), TAPS ** -0.5, 0.25, (), jnp.float32),
        "probes": scatter_about(own_keys[2], (P_SIZE, PROBES), 1.0, 6.0, ((0, 4), (1, 4)), jnp.float32),
    }


def reference(design, filter_taps, probes):
    highest = lax.Precision.HIGHEST
    projected = jnp.einsum('ctp,pk->ctk', design, probes, precision=highest)
    padding = jnp.zeros((COMP, TAPS - 1, PROBES), jnp.float32)
    padded = jnp.concatenate([padding, projected], axis=1)

    def forward(lag_step, running):
        segment = lax.dynamic_slice_in_dim(padded, TAPS - 1 - lag_step, EPOCHS, 1)
        coefficient = lax.dynamic_slice_in_dim(filter_taps, lag_step, 1, 1)
        return running + coefficient[:, :, None] * segment

    filtered = lax.fori_loop(0, TAPS, forward, jnp.zeros((COMP, EPOCHS, PROBES), jnp.float32))
    padded_after = jnp.concatenate([filtered, padding], axis=1)

    def backward(lag_step, running):
        segment = lax.dynamic_slice_in_dim(padded_after, lag_step, EPOCHS, 1)
        coefficient = lax.dynamic_slice_in_dim(filter_taps, lag_step, 1, 1)
        return running + coefficient[:, :, None] * segment

    weighted = lax.fori_loop(0, TAPS, backward, jnp.zeros((COMP, EPOCHS, PROBES), jnp.float32))
    return jnp.einsum('ctp,ctk->pk', design, weighted, precision=highest)
```

```python
import functools
import math

import jax
import jax.numpy as jnp
import numpy as np
from jax import lax
from jax.experimental import pallas as pl
from jax.experimental.pallas import tpu as pltpu
from jax.sharding import PartitionSpec as P


def passed_along(value, axis, by):
    length = lax.axis_size(axis)
    pairs = [(i, i + by) for i in range(length) if 0 <= i + by < length]
    return lax.ppermute(value, axis, pairs)


def block_taps(filter_taps, epochs, block_total, forward):
    shape = (block_total, epochs, epochs)
    distance = lax.broadcasted_iota(jnp.int32, shape, 0)
    source = lax.broadcasted_iota(jnp.int32, shape, 1)
    target = lax.broadcasted_iota(jnp.int32, shape, 2)
    if forward:
        lag_index = distance * epochs + target - source
    else:
        lag_index = distance * epochs + source - target
    tap_count = filter_taps.shape[1]
    inside = (lag_index >= 0) & (lag_index < tap_count)
    values = jnp.take(filter_taps, jnp.clip(lag_index, 0, tap_count - 1), axis=1)
    return jnp.where(inside[None], values, 0.0)


def apply_blocks(stacked, matrices):
    return jnp.einsum("ckdbe,cdef->ckbf", stacked, matrices, precision=lax.Precision.HIGHEST)


def body(design, filter_taps, probes):
    highest = lax.Precision.HIGHEST
    components, epochs, coefficients = design.shape
    tap_count = filter_taps.shape[1]
    blocks_back = (tap_count - 1 + epochs - 1) // epochs
    block_total = blocks_back + 1
    block_width = math.gcd(coefficients, 512)
    block_count = coefficients // block_width
    forward_taps = block_taps(filter_taps, epochs, block_total, True)
    backward_taps = block_taps(filter_taps, epochs, block_total, False)
    columns = lax.all_gather(probes, "tm", axis=1, tiled=True)

    def accumulate(step_index, running):
        start = step_index * block_width
        design_block = lax.dynamic_slice_in_dim(design, start, block_width, 2)
        column_block = lax.dynamic_slice_in_dim(columns, start, block_width, 0)
        return running + jnp.einsum("ctp,pk->ckt", design_block, column_block, precision=highest)

    initial = jnp.zeros((components, columns.shape[1], epochs), jnp.float32)
    projected = lax.fori_loop(0, block_count, accumulate, initial)
    projected = lax.psum_scatter(projected, "param", scatter_dimension=1, tiled=True)
    probe_count = projected.shape[1]
    before = [passed_along(projected, "tm", distance) for distance in range(blocks_back, 0, -1)]
    extended = jnp.stack(before + [projected], axis=2)
    pick_forward = np.array([[blocks_back - d] for d in range(block_total)], np.int32)
    filtered = apply_blocks(extended[:, :, pick_forward], forward_taps)
    filtered = filtered.reshape(components, probe_count, epochs)
    trailing = [passed_along(filtered, "tm", -distance) for distance in range(1, blocks_back + 1)]
    extended = jnp.stack([filtered] + trailing, axis=2)
    weighted = apply_blocks(extended[:, :, :, None], backward_taps)
    weighted = weighted.reshape(components, probe_count, epochs)
    weighted = lax.all_gather(weighted, "param", axis=1, tiled=True)

    def block_product(step_index):
        design_block = lax.dynamic_slice_in_dim(design, step_index * block_width, block_width, 2)
        return jnp.einsum("ctp,ckt->pk", design_block, weighted, precision=highest)

    stacked = lax.map(block_product, jnp.arange(block_count, dtype=jnp.int32))
    partial_value = stacked.reshape(coefficients, weighted.shape[1])
    result = lax.psum_scatter(partial_value, "tm", scatter_dimension=1, tiled=True)
    return result


CHUNK = 8
PIECES = 2
MESH = pl.DeviceIdType.MESH


def halves(value):
    high = value.astype(jnp.bfloat16)
    low = (value - high.astype(jnp.float32)).astype(jnp.bfloat16)
    return high, low


def across(left, right, precision=None):
    return lax.dot_general(left, right, (((1,), (1,)), ((), ())), precision=precision, preferred_element_type=jnp.float32)


def kernel(tm, param, components, design, taps, probes, out, raw, split, gathered, products, arrived, partials, signals,
           normal, blocks, load_sem, probe_sem, out_sem, a_send, a_recv, b_send, b_recv, p_send, p_recv, t_send, t_recv):
    rows, coefficients = raw.shape
    epochs = rows // components
    chunks = gathered.shape[0]
    piece = coefficients // PIECES
    z = lax.axis_index("tm")
    q = lax.axis_index("param")
    highest = lax.Precision.HIGHEST

    tile = math.gcd(coefficients, 2048)
    tiles = coefficients // tile
    loads = [pltpu.make_async_copy(design.at[:, pl.ds(j * tile, tile)], raw.at[:, pl.ds(j * tile, tile)], load_sem.at[j]) for j in range(tiles)]
    fetches = [pltpu.make_async_copy(probes.at[pl.ds(c * CHUNK, CHUNK)], gathered.at[c, z], probe_sem.at[c]) for c in range(chunks)]
    for copy in fetches + loads:
        copy.start()

    barrier = pltpu.get_barrier_semaphore()
    for by in range(1, tm):
        pl.semaphore_signal(barrier, inc=1, device_id={"tm": lax.rem(z + by, tm)}, device_id_type=MESH)
    for by in range(1, param):
        pl.semaphore_signal(barrier, inc=1, device_id={"param": lax.rem(q + by, param)}, device_id_type=MESH)
    pl.semaphore_wait(barrier, tm + param - 2)

    def place(way, index):
        return index if way == 0 else tm - 1 - index

    def message(step, way, h, sender, act):
        stage, slot = step // tm, step % tm
        d = slot - sender
        lanes = pl.ds(h * piece, piece)
        peer = {"tm": jnp.clip(place(way, sender + 1), 0, tm - 1)}
        there = (sender >= 0) & (sender < tm - 1)
        if stage < chunks:
            origin = jnp.clip(place(way, jnp.where(d < 0, -d, 0)), 0, tm - 1)

            @pl.when(there & ((d < 0) | (d == 1)))
            def _():
                block = gathered.at[stage, origin, :, lanes]
                copy = pltpu.make_async_remote_copy(
                    src_ref=block, dst_ref=block, send_sem=a_send.at[way, stage, h, origin],
                    recv_sem=a_recv.at[way, stage, h, origin], device_id=peer, device_id_type=MESH)
                act(copy, None)

        chunk = stage - 2
        if 0 <= chunk < chunks:
            owner = jnp.clip(place(way, jnp.where(d == 0, tm - 1, tm - d)), 0, tm - 1)

            @pl.when(there & ((d == 0) | (d >= 2)))
            def _():
                copy = pltpu.make_async_remote_copy(
                    src_ref=products.at[chunk, owner, :, lanes], dst_ref=arrived.at[way, chunk, owner, :, lanes],
                    send_sem=b_send.at[way, chunk, h, owner], recv_sem=b_recv.at[way, chunk, h, owner],
                    device_id=peer, device_id_type=MESH)

                def add():
                    products[chunk, owner, :, lanes] += arrived[way, chunk, owner, :, lanes]

                act(copy, add)

    def begin(copy, add):
        copy.start()

    def receive(copy, add):
        copy.wait_recv()
        if add is not None:
            add()

    def finish(copy, add):
        copy.wait_send()

    def prepare():
        total = tm * epochs
        source = lax.broadcasted_iota(jnp.int32, (total, total), 0)
        target = lax.broadcasted_iota(jnp.int32, (total, total), 1)
        blocks[...] = jnp.zeros_like(blocks)
        for c in range(components):
            row = jnp.broadcast_to(taps[c:c + 1, :total], (total, total))
            shifted = pltpu.roll(row, 0, 1, stride=1, stride_axis=0)
            shifted = jnp.where(target >= source, shifted, 0.0)
            normal[...] = across(shifted, shifted, highest)
            own = normal[pl.ds(pl.multiple_of(z * epochs, epochs), epochs), :]
            span = slice(c * epochs, (c + 1) * epochs)
            for other in range(tm):
                blocks[other, span, span] = own[:, other * epochs:(other + 1) * epochs]

    def convert():
        for copy in loads:
            copy.wait()

        @pl.loop(0, tiles)
        def _(j):
            lanes = pl.ds(pl.multiple_of(j * tile, tile), tile)
            high, low = halves(raw[:, lanes])
            split[:rows, lanes] = high
            split[rows:, lanes] = low

    def to_param(c, by):
        peer = {"param": lax.rem(q + by, param)}
        return pltpu.make_async_remote_copy(
            src_ref=partials.at[c, q], dst_ref=partials.at[c, q], send_sem=p_send.at[c, by],
            recv_sem=p_recv.at[c, by], device_id=peer, device_id_type=MESH)

    def to_tm(c, by):
        peer = {"tm": lax.rem(z + by, tm)}
        return pltpu.make_async_remote_copy(
            src_ref=signals.at[c, z], dst_ref=signals.at[c, z], send_sem=t_send.at[c, by],
            recv_sem=t_recv.at[c, by], device_id=peer, device_id_type=MESH)

    def project(c):
        columns = tm * CHUNK

        def add(j, running):
            lanes = pl.ds(pl.multiple_of(j * tile, tile), tile)
            high, low = halves(gathered[c, :, :, lanes].reshape(columns, tile))
            return running + across(jnp.concatenate([high, low], axis=0), split[:, lanes])

        full = lax.fori_loop(0, tiles, add, jnp.zeros((2 * columns, 2 * rows), jnp.float32))
        full = full[:columns] + full[columns:]
        partials[c, q] = full[:, :rows] + full[:, rows:]
        for by in range(1, param):
            to_param(c, by).start()

    def combine(c):
        for by in range(1, param):
            to_param(c, by).wait_recv()
        total = partials[c, 0]
        for other in range(1, param):
            total = total + partials[c, other]
        signals[c, z] = total
        for by in range(1, tm):
            to_tm(c, by).start()

    def expand(c):
        for by in range(1, tm):
            to_tm(c, by).wait_recv()
        weighted = across(signals[c, 0], blocks[0], highest)
        for other in range(1, tm):
            weighted = weighted + across(signals[c, other], blocks[other], highest)
        columns = tm * CHUNK
        high, low = halves(weighted)
        both = jnp.concatenate([high, low], axis=0)

        @pl.loop(0, tiles)
        def _(j):
            lanes = pl.ds(pl.multiple_of(j * tile, tile), tile)
            first = jnp.dot(both, split[:rows, lanes], preferred_element_type=jnp.float32)
            second = jnp.dot(high, split[rows:, lanes], preferred_element_type=jnp.float32)
            value = first[:columns] + first[columns:] + second
            products[c, :, :, lanes] = value.reshape(tm, CHUNK, tile)

    def write(c):
        return pltpu.make_async_copy(products.at[c, z], out.at[pl.ds(c * CHUNK, CHUNK)], out_sem.at[c])

    steps = (chunks + 2) * tm
    for step in range(steps + 1):
        stage, slot = step // tm, step % tm
        if slot == 0 and stage < chunks:
            fetches[stage].wait()
        for h in range(PIECES):
            for way in range(2):
                if step > 0:
                    message(step - 1, way, h, place(way, z) - 1, receive)
            for way in range(2):
                if step < steps:
                    message(step, way, h, place(way, z), begin)
        if slot == 0 and stage >= 3:
            write(stage - 3).start()
        if step == 0:
            prepare()
            convert()
        if 1 <= stage <= chunks:
            for unit, work in enumerate((project, combine, expand)):
                if slot == min(unit, tm - 1):
                    work(stage - 1)

    for step in range(steps):
        for h in range(PIECES):
            for way in range(2):
                message(step, way, h, place(way, z), finish)
    for c in range(chunks):
        for by in range(1, param):
            to_param(c, by).wait_send()
        for by in range(1, tm):
            to_tm(c, by).wait_send()
        write(c).wait()


def fused(tm, param, design, filter_taps, probes):
    components, epochs, coefficients = design.shape
    own = probes.shape[1]
    chunks = own // CHUNK
    rows = components * epochs
    columns = tm * CHUNK
    total = tm * epochs
    f32 = jnp.float32
    dma = pltpu.SemaphoreType.DMA
    flops = 8 * rows * coefficients * own * tm
    result = pl.pallas_call(
        functools.partial(kernel, tm, param, components),
        out_shape=jax.ShapeDtypeStruct((own, coefficients), f32),
        in_specs=[pl.BlockSpec(memory_space=pl.ANY), pl.BlockSpec(memory_space=pltpu.VMEM), pl.BlockSpec(memory_space=pl.ANY)],
        out_specs=pl.BlockSpec(memory_space=pl.ANY),
        scratch_shapes=[
            pltpu.VMEM((rows, coefficients), f32),
            pltpu.VMEM((2 * rows, coefficients), jnp.bfloat16),
            pltpu.VMEM((chunks, tm, CHUNK, coefficients), f32),
            pltpu.VMEM((chunks, tm, CHUNK, coefficients), f32),
            pltpu.VMEM((2, chunks, tm, CHUNK, coefficients), f32),
            pltpu.VMEM((chunks, param, columns, rows), f32),
            pltpu.VMEM((chunks, tm, columns, rows), f32),
            pltpu.VMEM((total, total), f32),
            pltpu.VMEM((tm, rows, rows), f32),
            dma((coefficients // math.gcd(coefficients, 2048),)),
            dma((chunks,)),
            dma((chunks,)),
            dma((2, chunks, PIECES, tm)),
            dma((2, chunks, PIECES, tm)),
            dma((2, chunks, PIECES, tm)),
            dma((2, chunks, PIECES, tm)),
            dma((chunks, param)),
            dma((chunks, param)),
            dma((chunks, tm)),
            dma((chunks, tm)),
        ],
        compiler_params=pltpu.CompilerParams(collective_id=0, has_side_effects=True, vmem_limit_bytes=56 * 1024 * 1024),
        cost_estimate=pl.CostEstimate(flops=flops, bytes_accessed=4 * coefficients * (rows + 2 * own), transcendentals=0),
    )(design.reshape(rows, coefficients), filter_taps, probes.T)
    return result.T


def solution(mesh):
    tm, param = mesh.shape["tm"], mesh.shape["param"]

    def run(design, filter_taps, probes):
        components, epochs, coefficients = design.shape
        held = 4 * coefficients * (2 * components * epochs + 4 * probes.shape[1] * tm)
        fits = held < 48 * 1024 * 1024 and tm * epochs <= min(filter_taps.shape[1], 512)
        if fits and tm > 2 and param > 1 and probes.shape[1] % CHUNK == 0 and epochs % 8 == 0 and coefficients % 256 == 0:
            return fused(tm, param, design, filter_taps, probes)
        return body(design, filter_taps, probes)

    in_specs = (P(None, ("groups", "tm"), "param"), P(), P("param", ("groups", "tm")))
    out_specs = P("param", ("groups", "tm"))
    return jax.shard_map(run, mesh=mesh, in_specs=in_specs, out_specs=out_specs, check_vma=False)
```

```python
import functools
import math

import jax
import jax.numpy as jnp
import numpy as np
from jax import lax
from jax.experimental import pallas as pl
from jax.experimental.pallas import tpu as pltpu
from jax.sharding import PartitionSpec as P


def passed_along(value, axis, by):
    length = lax.axis_size(axis)
    pairs = [(i, i + by) for i in range(length) if 0 <= i + by < length]
    return lax.ppermute(value, axis, pairs)


def block_taps(filter_taps, epochs, block_total, forward):
    shape = (block_total, epochs, epochs)
    distance = lax.broadcasted_iota(jnp.int32, shape, 0)
    source = lax.broadcasted_iota(jnp.int32, shape, 1)
    target = lax.broadcasted_iota(jnp.int32, shape, 2)
    if forward:
        lag_index = distance * epochs + target - source
    else:
        lag_index = distance * epochs + source - target
    tap_count = filter_taps.shape[1]
    inside = (lag_index >= 0) & (lag_index < tap_count)
    values = jnp.take(filter_taps, jnp.clip(lag_index, 0, tap_count - 1), axis=1)
    return jnp.where(inside[None], values, 0.0)


def apply_blocks(stacked, matrices):
    return jnp.einsum("ckdbe,cdef->ckbf", stacked, matrices, precision=lax.Precision.HIGHEST)


def body(design, filter_taps, probes):
    highest = lax.Precision.HIGHEST
    components, epochs, coefficients = design.shape
    tap_count = filter_taps.shape[1]
    blocks_back = (tap_count - 1 + epochs - 1) // epochs
    block_total = blocks_back + 1
    block_width = math.gcd(coefficients, 512)
    block_count = coefficients // block_width
    forward_taps = block_taps(filter_taps, epochs, block_total, True)
    backward_taps = block_taps(filter_taps, epochs, block_total, False)
    columns = lax.all_gather(probes, "tm", axis=1, tiled=True)

    def accumulate(step_index, running):
        start = step_index * block_width
        design_block = lax.dynamic_slice_in_dim(design, start, block_width, 2)
        column_block = lax.dynamic_slice_in_dim(columns, start, block_width, 0)
        return running + jnp.einsum("ctp,pk->ckt", design_block, column_block, precision=highest)

    initial = jnp.zeros((components, columns.shape[1], epochs), jnp.float32)
    projected = lax.fori_loop(0, block_count, accumulate, initial)
    projected = lax.psum_scatter(projected, "param", scatter_dimension=1, tiled=True)
    probe_count = projected.shape[1]
    before = [passed_along(projected, "tm", distance) for distance in range(blocks_back, 0, -1)]
    extended = jnp.stack(before + [projected], axis=2)
    pick_forward = np.array([[blocks_back - d] for d in range(block_total)], np.int32)
    filtered = apply_blocks(extended[:, :, pick_forward], forward_taps)
    filtered = filtered.reshape(components, probe_count, epochs)
    trailing = [passed_along(filtered, "tm", -distance) for distance in range(1, blocks_back + 1)]
    extended = jnp.stack([filtered] + trailing, axis=2)
    weighted = apply_blocks(extended[:, :, :, None], backward_taps)
    weighted = weighted.reshape(components, probe_count, epochs)
    weighted = lax.all_gather(weighted, "param", axis=1, tiled=True)

    def block_product(step_index):
        design_block = lax.dynamic_slice_in_dim(design, step_index * block_width, block_width, 2)
        return jnp.einsum("ctp,ckt->pk", design_block, weighted, precision=highest)

    stacked = lax.map(block_product, jnp.arange(block_count, dtype=jnp.int32))
    partial_value = stacked.reshape(coefficients, weighted.shape[1])
    result = lax.psum_scatter(partial_value, "tm", scatter_dimension=1, tiled=True)
    return result


CHUNK = 8
PIECES = 2
LAG = 2
TILE = 1024
MESH = pl.DeviceIdType.MESH


def halves(value):
    high = value.astype(jnp.bfloat16)
    low = (value - high.astype(jnp.float32)).astype(jnp.bfloat16)
    return high, low


def across(left, right, precision=None):
    return lax.dot_general(left, right, (((1,), (1,)), ((), ())), precision=precision, preferred_element_type=jnp.float32)


def plan(tm, chunks):
    links = tm - 1
    units = 2 * PIECES + 1
    todo = [[("a", c, h, i) for c in range(chunks) for h in range(PIECES) for i in range(link + 1)]
            + [("b", c, h, i) for c in range(chunks) for h in range(PIECES) for i in range(link + 1, tm)]
            for link in range(links)]
    sent = [{} for _ in range(links)]
    done = {}
    slots, work = [], []

    def rank(link, message):
        kind, c, h, i = message
        if kind == "a":
            return 2 * c - 2 * (links - 1 - i) + link - i
        return 5 + 8 * c - i + 2 * link

    def passed(link, message, now):
        return message in sent[link] and sent[link][message] + LAG <= now

    def ready(link, message, now):
        kind, c, h, i = message
        if kind == "a":
            return i == link or passed(link - 1, message, now)
        return done.get((c, PIECES + 1 + h), now) < now and (link == 0 or passed(link - 1, message, now))

    def possible(c, unit, now):
        if (c, unit) in done or (unit > 0 and done.get((c, unit - 1), now) >= now):
            return False
        if unit >= PIECES:
            return True
        return all(passed(link, ("a", c, unit, i), now) for link in range(links) for i in range(link + 1))

    while any(todo):
        now = len(slots)
        row = []
        for link in range(links):
            choice = [(rank(link, m), m) for m in todo[link] if ready(link, m, now)]
            row.append(min(choice)[1] if choice else None)
        for link, message in enumerate(row):
            if message is not None:
                sent[link][message] = now
                todo[link].remove(message)
        choice = [(c, unit) for c in range(chunks) for unit in range(units) if possible(c, unit, now)]
        if choice:
            done[min(choice)] = now
        slots.append(row)
        work.append(min(choice) if choice else None)
    return slots, work


def kernel(tm, param, components, design, taps, probes, out, raw, split, gathered, products, arrived, partials, signals,
           weights, normal, blocks, load_sem, probe_sem, out_sem, a_send, a_recv, b_send, b_recv, p_send, p_recv, t_send,
           t_recv):
    rows, coefficients = raw.shape
    epochs = rows // components
    chunks = gathered.shape[0]
    columns = tm * CHUNK
    piece = coefficients // PIECES
    z = lax.axis_index("tm")
    q = lax.axis_index("param")
    highest = lax.Precision.HIGHEST
    slots, work = plan(tm, chunks)

    tile = math.gcd(piece, TILE)
    tiles = coefficients // tile
    steps_each = piece // tile
    loads = [pltpu.make_async_copy(design.at[:, pl.ds(h * piece, piece)], raw.at[:, pl.ds(h * piece, piece)], load_sem.at[h]) for h in range(PIECES)]
    fetches = [pltpu.make_async_copy(probes.at[pl.ds(c * CHUNK, CHUNK)], gathered.at[c, z], probe_sem.at[c]) for c in range(chunks)]
    for copy in fetches + loads:
        copy.start()

    barrier = pltpu.get_barrier_semaphore()
    for by in range(1, tm):
        pl.semaphore_signal(barrier, inc=1, device_id={"tm": lax.rem(z + by, tm)}, device_id_type=MESH)
    for by in range(1, param):
        pl.semaphore_signal(barrier, inc=1, device_id={"param": lax.rem(q + by, param)}, device_id_type=MESH)
    pl.semaphore_wait(barrier, tm + param - 2)

    def place(way, index):
        return index if way == 0 else tm - 1 - index

    def transfer(way, link, message):
        kind, c, h, i = message
        lanes = pl.ds(h * piece, piece)
        i = place(way, i)
        if kind == "a":
            source = target = gathered.at[c, i, :, lanes]
            sems = a_send.at[way, c, h, i], a_recv.at[way, c, h, i]
        else:
            source, target = products.at[c, i, :, lanes], arrived.at[way, c, i, :, lanes]
            sems = b_send.at[way, c, h, i], b_recv.at[way, c, h, i]
        return pltpu.make_async_remote_copy(
            src_ref=source, dst_ref=target, send_sem=sems[0], recv_sem=sems[1],
            device_id={"tm": place(way, link + 1)}, device_id_type=MESH)

    def each(row, act, ahead):
        for way in range(2):
            for link, message in enumerate(row):
                if message is not None:
                    pl.when(z == place(way, link + ahead))(functools.partial(act, way, link, message))

    def begin(way, link, message):
        transfer(way, link, message).start()

    def finish(way, link, message):
        transfer(way, link, message).wait_send()

    def receive(way, link, message):
        transfer(way, link, message).wait_recv()
        kind, c, h, i = message
        if kind == "b":
            lanes = pl.ds(h * piece, piece)
            i = place(way, i)
            products[c, i, :, lanes] += arrived[way, c, i, :, lanes]

    def prepare(c):
        total = tm * epochs
        source = lax.broadcasted_iota(jnp.int32, (total, total), 0)
        target = lax.broadcasted_iota(jnp.int32, (total, total), 1)
        if c == 0:
            blocks[...] = jnp.zeros_like(blocks)
        row = jnp.broadcast_to(taps[c:c + 1, :total], (total, total))
        shifted = pltpu.roll(row, 0, 1, stride=1, stride_axis=0)
        shifted = jnp.where(target >= source, shifted, 0.0)
        normal[...] = across(shifted, shifted, highest)
        own = normal[pl.ds(pl.multiple_of(z * epochs, epochs), epochs), :]
        span = slice(c * epochs, (c + 1) * epochs)
        for other in range(tm):
            blocks[other, span, span] = own[:, other * epochs:(other + 1) * epochs]

    def convert():
        for copy in loads:
            copy.wait()

        @pl.loop(0, tiles)
        def _(j):
            lanes = pl.ds(pl.multiple_of(j * tile, tile), tile)
            high, low = halves(raw[:, lanes])
            split[:rows, lanes] = high
            split[rows:, lanes] = low

    def to_param(c, by):
        peer = {"param": lax.rem(q + by, param)}
        return pltpu.make_async_remote_copy(
            src_ref=partials.at[c, q], dst_ref=partials.at[c, q], send_sem=p_send.at[c, by],
            recv_sem=p_recv.at[c, by], device_id=peer, device_id_type=MESH)

    def to_tm(c, by):
        peer = {"tm": lax.rem(z + by, tm)}
        return pltpu.make_async_remote_copy(
            src_ref=signals.at[c, z], dst_ref=signals.at[c, z], send_sem=t_send.at[c, by],
            recv_sem=t_recv.at[c, by], device_id=peer, device_id_type=MESH)

    def project(c, h):
        def add(j, running):
            lanes = pl.ds(pl.multiple_of(j * tile, tile), tile)
            high, low = halves(gathered[c, :, :, lanes].reshape(columns, tile))
            return running + across(jnp.concatenate([high, low], axis=0), split[:, lanes])

        full = jnp.zeros((2 * columns, 2 * rows), jnp.float32)
        full = lax.fori_loop(h * steps_each, (h + 1) * steps_each, add, full)
        full = full[:columns] + full[columns:]
        value = full[:, :rows] + full[:, rows:]
        partials[c, q] = value if h == 0 else partials[c, q] + value
        if h == PIECES - 1:
            for by in range(1, param):
                to_param(c, by).start()

    def combine(c):
        for by in range(1, param):
            to_param(c, by).wait_recv()
        total = partials[c, 0]
        for other in range(1, param):
            total = total + partials[c, other]
        signals[c, z] = total
        for by in range(1, tm):
            to_tm(c, by).start()

    def expand(c, h):
        if h == 0:
            for by in range(1, tm):
                to_tm(c, by).wait_recv()
            weighted = across(signals[c, 0], blocks[0], highest)
            for other in range(1, tm):
                weighted = weighted + across(signals[c, other], blocks[other], highest)
            high, low = halves(weighted)
            weights[...] = jnp.concatenate([high, low], axis=0)

        @pl.loop(h * steps_each, (h + 1) * steps_each)
        def _(j):
            lanes = pl.ds(pl.multiple_of(j * tile, tile), tile)
            first = jnp.dot(weights[...], split[:rows, lanes], preferred_element_type=jnp.float32)
            second = jnp.dot(weights[:columns], split[rows:, lanes], preferred_element_type=jnp.float32)
            value = first[:columns] + first[columns:] + second
            products[c, :, :, lanes] = value.reshape(tm, CHUNK, tile)

    def write(c):
        return pltpu.make_async_copy(products.at[c, z], out.at[pl.ds(c * CHUNK, CHUNK)], out_sem.at[c])

    own_first = [min(g for g, row in enumerate(slots) if any(m is not None and m[:2] == ("a", c) for m in row)) for c in range(chunks)]
    last = [max(g for g, row in enumerate(slots) if any(m is not None and m[:2] == ("b", c) for m in row)) for c in range(chunks)]
    for step in range(len(slots) + LAG):
        for c in range(chunks):
            if own_first[c] == step:
                fetches[c].wait()
        if step >= LAG:
            each(slots[step - LAG], receive, 1)
        if step < len(slots):
            each(slots[step], begin, 0)
        for c in range(chunks):
            if last[c] + LAG == step:
                write(c).start()
        if step == 0:
            convert()
        elif step <= components:
            prepare(step - 1)
        if step < len(slots) and work[step] is not None:
            c, unit = work[step]
            if unit < PIECES:
                project(c, unit)
            elif unit == PIECES:
                combine(c)
            else:
                expand(c, unit - PIECES - 1)

    for row in slots:
        each(row, finish, 0)
    for c in range(chunks):
        for by in range(1, param):
            to_param(c, by).wait_send()
        for by in range(1, tm):
            to_tm(c, by).wait_send()
        write(c).wait()


def fused(tm, param, design, filter_taps, probes):
    components, epochs, coefficients = design.shape
    own = probes.shape[1]
    chunks = own // CHUNK
    rows = components * epochs
    columns = tm * CHUNK
    total = tm * epochs
    f32 = jnp.float32
    dma = pltpu.SemaphoreType.DMA
    flops = 8 * rows * coefficients * own * tm
    result = pl.pallas_call(
        functools.partial(kernel, tm, param, components),
        out_shape=jax.ShapeDtypeStruct((own, coefficients), f32),
        in_specs=[pl.BlockSpec(memory_space=pl.ANY), pl.BlockSpec(memory_space=pltpu.VMEM), pl.BlockSpec(memory_space=pl.ANY)],
        out_specs=pl.BlockSpec(memory_space=pl.ANY),
        scratch_shapes=[
            pltpu.VMEM((rows, coefficients), f32),
            pltpu.VMEM((2 * rows, coefficients), jnp.bfloat16),
            pltpu.VMEM((chunks, tm, CHUNK, coefficients), f32),
            pltpu.VMEM((chunks, tm, CHUNK, coefficients), f32),
            pltpu.VMEM((2, chunks, tm, CHUNK, coefficients), f32),
            pltpu.VMEM((chunks, param, columns, rows), f32),
            pltpu.VMEM((chunks, tm, columns, rows), f32),
            pltpu.VMEM((2 * columns, rows), jnp.bfloat16),
            pltpu.VMEM((total, total), f32),
            pltpu.VMEM((tm, rows, rows), f32),
            dma((PIECES,)),
            dma((chunks,)),
            dma((chunks,)),
            dma((2, chunks, PIECES, tm)),
            dma((2, chunks, PIECES, tm)),
            dma((2, chunks, PIECES, tm)),
            dma((2, chunks, PIECES, tm)),
            dma((chunks, param)),
            dma((chunks, param)),
            dma((chunks, tm)),
            dma((chunks, tm)),
        ],
        compiler_params=pltpu.CompilerParams(collective_id=0, has_side_effects=True, vmem_limit_bytes=56 * 1024 * 1024),
        cost_estimate=pl.CostEstimate(flops=flops, bytes_accessed=4 * coefficients * (rows + 2 * own), transcendentals=0),
    )(design.reshape(rows, coefficients), filter_taps, probes.T)
    return result.T


def solution(mesh):
    tm, param = mesh.shape["tm"], mesh.shape["param"]

    def run(design, filter_taps, probes):
        components, epochs, coefficients = design.shape
        held = 4 * coefficients * (2 * components * epochs + 4 * probes.shape[1] * tm)
        fits = held < 48 * 1024 * 1024 and tm * epochs <= min(filter_taps.shape[1], 512)
        if fits and tm > 2 and param > 1 and probes.shape[1] % CHUNK == 0 and epochs % 8 == 0 and coefficients % 256 == 0:
            return fused(tm, param, design, filter_taps, probes)
        return body(design, filter_taps, probes)

    in_specs = (P(None, ("groups", "tm"), "param"), P(), P("param", ("groups", "tm")))
    out_specs = P("param", ("groups", "tm"))
    return jax.shard_map(run, mesh=mesh, in_specs=in_specs, out_specs=out_specs, check_vma=False)
```

```python
import functools
import math

import jax
import jax.numpy as jnp
import numpy as np
from jax import lax
from jax.experimental import pallas as pl
from jax.experimental.pallas import tpu as pltpu
from jax.sharding import PartitionSpec as P


def passed_along(value, axis, by):
    length = lax.axis_size(axis)
    pairs = [(i, i + by) for i in range(length) if 0 <= i + by < length]
    return lax.ppermute(value, axis, pairs)


def block_taps(filter_taps, epochs, block_total, forward):
    shape = (block_total, epochs, epochs)
    distance = lax.broadcasted_iota(jnp.int32, shape, 0)
    source = lax.broadcasted_iota(jnp.int32, shape, 1)
    target = lax.broadcasted_iota(jnp.int32, shape, 2)
    if forward:
        lag_index = distance * epochs + target - source
    else:
        lag_index = distance * epochs + source - target
    tap_count = filter_taps.shape[1]
    inside = (lag_index >= 0) & (lag_index < tap_count)
    values = jnp.take(filter_taps, jnp.clip(lag_index, 0, tap_count - 1), axis=1)
    return jnp.where(inside[None], values, 0.0)


def apply_blocks(stacked, matrices):
    return jnp.einsum("ckdbe,cdef->ckbf", stacked, matrices, precision=lax.Precision.HIGHEST)


def body(design, filter_taps, probes):
    highest = lax.Precision.HIGHEST
    components, epochs, coefficients = design.shape
    tap_count = filter_taps.shape[1]
    blocks_back = (tap_count - 1 + epochs - 1) // epochs
    block_total = blocks_back + 1
    block_width = math.gcd(coefficients, 512)
    block_count = coefficients // block_width
    forward_taps = block_taps(filter_taps, epochs, block_total, True)
    backward_taps = block_taps(filter_taps, epochs, block_total, False)
    columns = lax.all_gather(probes, "tm", axis=1, tiled=True)

    def accumulate(step_index, running):
        start = step_index * block_width
        design_block = lax.dynamic_slice_in_dim(design, start, block_width, 2)
        column_block = lax.dynamic_slice_in_dim(columns, start, block_width, 0)
        return running + jnp.einsum("ctp,pk->ckt", design_block, column_block, precision=highest)

    initial = jnp.zeros((components, columns.shape[1], epochs), jnp.float32)
    projected = lax.fori_loop(0, block_count, accumulate, initial)
    projected = lax.psum_scatter(projected, "param", scatter_dimension=1, tiled=True)
    probe_count = projected.shape[1]
    before = [passed_along(projected, "tm", distance) for distance in range(blocks_back, 0, -1)]
    extended = jnp.stack(before + [projected], axis=2)
    pick_forward = np.array([[blocks_back - d] for d in range(block_total)], np.int32)
    filtered = apply_blocks(extended[:, :, pick_forward], forward_taps)
    filtered = filtered.reshape(components, probe_count, epochs)
    trailing = [passed_along(filtered, "tm", -distance) for distance in range(1, blocks_back + 1)]
    extended = jnp.stack([filtered] + trailing, axis=2)
    weighted = apply_blocks(extended[:, :, :, None], backward_taps)
    weighted = weighted.reshape(components, probe_count, epochs)
    weighted = lax.all_gather(weighted, "param", axis=1, tiled=True)

    def block_product(step_index):
        design_block = lax.dynamic_slice_in_dim(design, step_index * block_width, block_width, 2)
        return jnp.einsum("ctp,ckt->pk", design_block, weighted, precision=highest)

    stacked = lax.map(block_product, jnp.arange(block_count, dtype=jnp.int32))
    partial_value = stacked.reshape(coefficients, weighted.shape[1])
    result = lax.psum_scatter(partial_value, "tm", scatter_dimension=1, tiled=True)
    return result


CHUNK = 8
PIECES = 4
LAG = 4
GAPS = 1, 3, 1
TILE = 1280
WA = 2, -2, 1
WB = 5, 8, -1, 2
MESH = pl.DeviceIdType.MESH


def halves(value):
    high = value.astype(jnp.bfloat16)
    low = (value - high.astype(jnp.float32)).astype(jnp.bfloat16)
    return high, low


def across(left, right, precision=None):
    return lax.dot_general(left, right, (((1,), (1,)), ((), ())), precision=precision, preferred_element_type=jnp.float32)


def plan(tm, chunks):
    links = tm - 1
    units = 2 * PIECES + 2
    todo = [[("a", c, h, i) for c in range(chunks) for h in range(PIECES) for i in range(link + 1)]
            + [("b", c, h, i) for c in range(chunks) for h in range(PIECES) for i in range(link + 1, tm)]
            for link in range(links)]
    sent = [{} for _ in range(links)]
    done = {}
    slots, work = [], []

    def rank(link, message):
        kind, c, h, i = message
        if kind == "a":
            return WA[0] * c + WA[1] * (links - 1 - i) + WA[2] * (link - i)
        return WB[0] + WB[1] * c + WB[2] * i + WB[3] * link

    def passed(link, message, now):
        return message in sent[link] and sent[link][message] + LAG <= now

    def ready(link, message, now):
        kind, c, h, i = message
        if kind == "a":
            return i == link or passed(link - 1, message, now)
        return done.get((c, PIECES + 2 + h), now) < now and (link == 0 or passed(link - 1, message, now))

    def possible(c, unit, now):
        wait = GAPS[unit - PIECES] if PIECES <= unit <= PIECES + 2 else 1
        if (c, unit) in done or (unit > 0 and done.get((c, unit - 1), now) + wait > now):
            return False
        if unit >= PIECES:
            return True
        return all(passed(link, ("a", c, unit, i), now) for link in range(links) for i in range(link + 1))

    while any(todo):
        now = len(slots)
        row = []
        for link in range(links):
            choice = [(rank(link, m), m) for m in todo[link] if ready(link, m, now)]
            row.append(min(choice)[1] if choice else None)
        for link, message in enumerate(row):
            if message is not None:
                sent[link][message] = now
                todo[link].remove(message)
        choice = [(c, unit) for c in range(chunks) for unit in range(units) if possible(c, unit, now)]
        if choice:
            done[min(choice)] = now
        slots.append(row)
        work.append(min(choice) if choice else None)
    return slots, work


def kernel(tm, param, components, design, taps, probes, out, raw, split, gathered, products, arrived, mine, partials,
           signals, filtered, weights, normal, blocks, load_sem, probe_sem, out_sem, z_send, z_recv, p_send, p_recv, t_send,
           t_recv, f_send, f_recv):
    rows, coefficients = raw.shape
    epochs = rows // components
    chunks = gathered.shape[0]
    columns = tm * CHUNK
    share = columns // param
    piece = coefficients // PIECES
    z = lax.axis_index("tm")
    q = lax.axis_index("param")
    highest = lax.Precision.HIGHEST
    slots, work = plan(tm, chunks)

    tile = math.gcd(piece, TILE)
    tiles = coefficients // tile
    steps_each = piece // tile
    loads = [pltpu.make_async_copy(design.at[:, pl.ds(h * piece, piece)], raw.at[:, pl.ds(h * piece, piece)], load_sem.at[h]) for h in range(PIECES)]
    fetches = [pltpu.make_async_copy(probes.at[pl.ds(c * CHUNK, CHUNK)], gathered.at[c, z], probe_sem.at[c]) for c in range(chunks)]
    for copy in fetches + loads:
        copy.start()

    barrier = pltpu.get_barrier_semaphore()
    for by in range(1, tm):
        pl.semaphore_signal(barrier, inc=1, device_id={"tm": lax.rem(z + by, tm)}, device_id_type=MESH)
    for by in range(1, param):
        pl.semaphore_signal(barrier, inc=1, device_id={"param": lax.rem(q + by, param)}, device_id_type=MESH)
    pl.semaphore_wait(barrier, tm + param - 2)

    def place(way, index):
        return index if way == 0 else tm - 1 - index

    def transfer(way, link, message):
        kind, c, h, i = message
        lanes = pl.ds(h * piece, piece)
        i = place(way, i)
        if kind == "a":
            source = target = gathered.at[c, i, :, lanes]
        else:
            source, target = products.at[c, i, :, lanes], arrived.at[way, c, i, :, lanes]
        return pltpu.make_async_remote_copy(
            src_ref=source, dst_ref=target, send_sem=z_send.at[way, c, h, i], recv_sem=z_recv.at[way, c, h, i],
            device_id={"tm": place(way, link + 1)}, device_id_type=MESH)

    def each(row, act, ahead):
        for way in range(2):
            for link, message in enumerate(row):
                if message is not None:
                    pl.when(z == place(way, link + ahead))(functools.partial(act, way, link, message))

    def begin(way, link, message):
        transfer(way, link, message).start()

    def finish(way, link, message):
        transfer(way, link, message).wait_send()

    def receive(way, link, message):
        transfer(way, link, message).wait_recv()
        kind, c, h, i = message
        if kind == "b":
            lanes = pl.ds(h * piece, piece)
            i = place(way, i)
            products[c, i, :, lanes] += arrived[way, c, i, :, lanes]

    def prepare(c):
        total = tm * epochs
        source = lax.broadcasted_iota(jnp.int32, (total, total), 0)
        target = lax.broadcasted_iota(jnp.int32, (total, total), 1)
        if c == 0:
            blocks[...] = jnp.zeros_like(blocks)
        row = jnp.broadcast_to(taps[c:c + 1, :total], (total, total))
        shifted = pltpu.roll(row, 0, 1, stride=1, stride_axis=0)
        shifted = jnp.where(target >= source, shifted, 0.0)
        normal[...] = across(shifted, shifted, highest)
        own = normal[pl.ds(pl.multiple_of(z * epochs, epochs), epochs), :]
        span = slice(c * epochs, (c + 1) * epochs)
        for other in range(tm):
            blocks[other, span, span] = own[:, other * epochs:(other + 1) * epochs]

    def convert():
        for copy in loads:
            copy.wait()

        @pl.loop(0, tiles)
        def _(j):
            lanes = pl.ds(pl.multiple_of(j * tile, tile), tile)
            high, low = halves(raw[:, lanes])
            split[:rows, lanes] = high
            split[rows:, lanes] = low

    def to_param(c, by):
        other = lax.rem(q + by, param)
        return pltpu.make_async_remote_copy(
            src_ref=mine.at[c, other], dst_ref=partials.at[c, q], send_sem=p_send.at[c, by],
            recv_sem=p_recv.at[c, by], device_id={"param": other}, device_id_type=MESH)

    def to_all(c, by):
        peer = {"param": lax.rem(q + by, param)}
        return pltpu.make_async_remote_copy(
            src_ref=filtered.at[c, q], dst_ref=filtered.at[c, q], send_sem=f_send.at[c, by],
            recv_sem=f_recv.at[c, by], device_id=peer, device_id_type=MESH)

    def to_tm(c, by):
        peer = {"tm": lax.rem(z + by, tm)}
        return pltpu.make_async_remote_copy(
            src_ref=signals.at[c, z], dst_ref=signals.at[c, z], send_sem=t_send.at[c, by],
            recv_sem=t_recv.at[c, by], device_id=peer, device_id_type=MESH)

    def project(c, h):
        def add(j, running):
            lanes = pl.ds(pl.multiple_of(j * tile, tile), tile)
            high, low = halves(gathered[c, :, :, lanes].reshape(columns, tile))
            return running + across(jnp.concatenate([high, low], axis=0), split[:, lanes])

        full = jnp.zeros((2 * columns, 2 * rows), jnp.float32)
        full = lax.fori_loop(h * steps_each, (h + 1) * steps_each, add, full)
        full = full[:columns] + full[columns:]
        value = (full[:, :rows] + full[:, rows:]).reshape(param, share, rows)
        mine[c] = value if h == 0 else mine[c] + value
        if h == PIECES - 1:
            partials[c, q] = mine[c, q]
            for by in range(1, param):
                to_param(c, by).start()

    def combine(c):
        for by in range(1, param):
            to_param(c, by).wait_recv()
        total = partials[c, 0]
        for other in range(1, param):
            total = total + partials[c, other]
        signals[c, z] = total
        for by in range(1, tm):
            to_tm(c, by).start()

    def weigh(c):
        for by in range(1, tm):
            to_tm(c, by).wait_recv()
        weighted = across(signals[c, 0], blocks[0], highest)
        for other in range(1, tm):
            weighted = weighted + across(signals[c, other], blocks[other], highest)
        filtered[c, q] = weighted
        for by in range(1, param):
            to_all(c, by).start()

    def expand(c, h):
        if h == 0:
            for by in range(1, param):
                to_all(c, by).wait_recv()
            high, low = halves(filtered[c].reshape(columns, rows))
            weights[...] = jnp.concatenate([high, low], axis=0)

        @pl.loop(h * steps_each, (h + 1) * steps_each)
        def _(j):
            lanes = pl.ds(pl.multiple_of(j * tile, tile), tile)
            first = jnp.dot(weights[...], split[:rows, lanes], preferred_element_type=jnp.float32)
            second = jnp.dot(weights[:columns], split[rows:, lanes], preferred_element_type=jnp.float32)
            value = first[:columns] + first[columns:] + second
            products[c, :, :, lanes] = value.reshape(tm, CHUNK, tile)

    def write(c):
        return pltpu.make_async_copy(products.at[c, z], out.at[pl.ds(c * CHUNK, CHUNK)], out_sem.at[c])

    own_first = [min(g for g, row in enumerate(slots) if any(m is not None and m[:2] == ("a", c) for m in row)) for c in range(chunks)]
    last = [max(g for g, row in enumerate(slots) if any(m is not None and m[:2] == ("b", c) for m in row)) for c in range(chunks)]
    for step in range(len(slots) + LAG):
        for c in range(chunks):
            if own_first[c] == step:
                fetches[c].wait()
        if step >= LAG:
            each(slots[step - LAG], receive, 1)
        if step < len(slots):
            each(slots[step], begin, 0)
        if step >= LAG:
            each(slots[step - LAG], finish, 0)
        for c in range(chunks):
            if last[c] + LAG == step:
                write(c).start()
        if step == 0:
            convert()
        elif step <= components:
            prepare(step - 1)
        if step < len(slots) and work[step] is not None:
            c, unit = work[step]
            if unit < PIECES:
                project(c, unit)
            elif unit == PIECES:
                combine(c)
            elif unit == PIECES + 1:
                weigh(c)
            else:
                expand(c, unit - PIECES - 2)
    for c in range(chunks):
        for by in range(1, param):
            to_param(c, by).wait_send()
            to_all(c, by).wait_send()
        for by in range(1, tm):
            to_tm(c, by).wait_send()
        write(c).wait()


def fused(tm, param, design, filter_taps, probes):
    components, epochs, coefficients = design.shape
    own = probes.shape[1]
    chunks = own // CHUNK
    rows = components * epochs
    columns = tm * CHUNK
    share = columns // param
    total = tm * epochs
    f32 = jnp.float32
    dma = pltpu.SemaphoreType.DMA
    flops = 8 * rows * coefficients * own * tm
    result = pl.pallas_call(
        functools.partial(kernel, tm, param, components),
        out_shape=jax.ShapeDtypeStruct((own, coefficients), f32),
        in_specs=[pl.BlockSpec(memory_space=pl.ANY), pl.BlockSpec(memory_space=pltpu.VMEM), pl.BlockSpec(memory_space=pl.ANY)],
        out_specs=pl.BlockSpec(memory_space=pl.ANY),
        scratch_shapes=[
            pltpu.VMEM((rows, coefficients), f32),
            pltpu.VMEM((2 * rows, coefficients), jnp.bfloat16),
            pltpu.VMEM((chunks, tm, CHUNK, coefficients), f32),
            pltpu.VMEM((chunks, tm, CHUNK, coefficients), f32),
            pltpu.VMEM((2, chunks, tm, CHUNK, coefficients), f32),
            pltpu.VMEM((chunks, param, share, rows), f32),
            pltpu.VMEM((chunks, param, share, rows), f32),
            pltpu.VMEM((chunks, tm, share, rows), f32),
            pltpu.VMEM((chunks, param, share, rows), f32),
            pltpu.VMEM((2 * columns, rows), jnp.bfloat16),
            pltpu.VMEM((total, total), f32),
            pltpu.VMEM((tm, rows, rows), f32),
            dma((PIECES,)),
            dma((chunks,)),
            dma((chunks,)),
            dma((2, chunks, PIECES, tm)),
            dma((2, chunks, PIECES, tm)),
            dma((chunks, param)),
            dma((chunks, param)),
            dma((chunks, tm)),
            dma((chunks, tm)),
            dma((chunks, param)),
            dma((chunks, param)),
        ],
        compiler_params=pltpu.CompilerParams(collective_id=0, has_side_effects=True, vmem_limit_bytes=56 * 1024 * 1024),
        cost_estimate=pl.CostEstimate(flops=flops, bytes_accessed=4 * coefficients * (rows + 2 * own), transcendentals=0),
    )(design.reshape(rows, coefficients), filter_taps, probes.T)
    return result.T


def solution(mesh):
    tm, param = mesh.shape["tm"], mesh.shape["param"]

    def run(design, filter_taps, probes):
        components, epochs, coefficients = design.shape
        held = 4 * coefficients * (2 * components * epochs + 4 * probes.shape[1] * tm)
        fits = held < 48 * 1024 * 1024 and tm * epochs <= min(filter_taps.shape[1], 512)
        if fits and tm > 2 and param > 1 and probes.shape[1] % CHUNK == 0 and epochs % 8 == 0 and coefficients % (128 * PIECES) == 0 and tm * CHUNK % (8 * param) == 0:
            return fused(tm, param, design, filter_taps, probes)
        return body(design, filter_taps, probes)

    in_specs = (P(None, ("groups", "tm"), "param"), P(), P("param", ("groups", "tm")))
    out_specs = P("param", ("groups", "tm"))
    return jax.shard_map(run, mesh=mesh, in_specs=in_specs, out_specs=out_specs, check_vma=False)
```
